256 devices in a mesh: patch: 32 (over z, y_lo, core), head: 8 (over x, y_hi).
Axes of the slice: x: 4, y: 4 (y_hi: 2, y_lo: 2; y = y_hi * 2 + y_lo), z: 8, core: 2. Of those that a mesh axis runs over, the one named last changes fastest.
Arguments:
- fresh_q: bfloat16 [12288, 3072], P(('patch', 'head')), may hold values from -180 to 180
- fresh_k: bfloat16 [12288, 3072], P(('patch', 'head')), may hold values from -180 to 180
- fresh_v: bfloat16 [12288, 3072], P(('patch', 'head')), may hold values from -6 to 6
- stale_k: bfloat16 [12288, 3072], P('patch', 'head'), may hold values from -20 to 20
- stale_v: bfloat16 [12288, 3072], P('patch', 'head'), may hold values from -6 to 6
- q_gain: float32 [3072], replicated, may hold values from 0.1 to 1.9
- k_gain: float32 [3072], replicated, may hold values from 0.1 to 1.9
Outputs:
- attended: bfloat16 [12288, 3072], P(('patch', 'head'))
- key_cache: bfloat16 [12288, 3072], P('patch', 'head')
The draws below stay inside these ranges and needn't reach their ends.
All inputs are finite; a program needn't handle non-finite values.
Results may differ from the reference program's by a relative error of at most 0.011.
Values may be sent and summed in bfloat16 or wider, within the bound.
No kernel may reach another device: no remote copies, remote signals or barrier semaphores. Data moves between devices by JAX's collectives and lax.ppermute only.
A program may use at most 192 MiB of HBM per device.

```python
import math
import jax
import jax.numpy as jnp
from jax import lax

HEADS = 24
HD = 128
TOK_PATCH = 384
TOKENS = 12288
N_PATCH = 32


def apply_scales(key, base_draw):
    subkeys = jax.random.split(key, 2)
    width_all = HEADS * HD
    row_scale = jnp.exp(jax.random.uniform(subkeys[0], (TOKENS, 1), jnp.float32, 0.0, math.log(10.0)))
    col_scale = jnp.exp(jax.random.uniform(subkeys[1], (1, width_all), jnp.float32, 0.0, math.log(10.0)))
    rising = 1.0 + 2.0 * (jnp.arange(width_all) // HD).astype(jnp.float32) / max(HEADS - 1, 1)
    return base_draw * row_scale * col_scale * rising[None, :] / 10.0


def draw_fresh_q(key, part):
    key = jax.random.fold_in(key, 11)
    subkeys = jax.random.split(key, 2)
    base_draw = jnp.clip(jax.random.normal(subkeys[0], (TOKENS, HEADS * HD), jnp.float32), -6.0, 6.0)
    drawn = apply_scales(subkeys[1], base_draw)
    return drawn.astype(jnp.bfloat16)


def draw_fresh_k(key, part):
    key = jax.random.fold_in(key, 12)
    subkeys = jax.random.split(key, 2)
    base_draw = jnp.clip(jax.random.normal(subkeys[0], (TOKENS, HEADS * HD), jnp.float32), -6.0, 6.0)
    return apply_scales(subkeys[1], base_draw).astype(jnp.bfloat16)


def draw_stale_k(key, part):
    key = jax.random.fold_in(key, 13)
    drawn = jnp.clip(jax.random.normal(key, (TOKENS, HEADS * HD), jnp.float32), -6.0, 6.0)
    return drawn.astype(jnp.bfloat16)


def level_of(stream_key, dims, cuts, least, high):
    factor_of, own = 1.0, jax.random.fold_in(stream_key, 6)
    for position, shards_of in cuts:
        draws = jnp.exp(jax.random.uniform(jax.random.fold_in(own, position), (shards_of,), jnp.float32, least / len(cuts), high / len(cuts)))
        factor_of = factor_of * jnp.repeat(draws, dims[position] // shards_of).reshape([-1 if axis == position else 1 for axis in range(len(dims))])
    return factor_of


def centred(key, extent, spread, bound, shards=(), kind=jnp.bfloat16):
    values = spread * jax.random.normal(key, extent, jnp.float32)
    if shards:
        values = values * level_of(key, extent, shards, -0.22, 0.18)
    return jnp.clip(values, -bound, bound).astype(kind)


def setup_inputs(seed: int = 0) -> dict:
    keys = jax.random.split(jax.random.key(seed), 8)
    fresh_q = draw_fresh_q(jax.random.fold_in(keys[7], 71), 0)
    fresh_k = draw_fresh_k(jax.random.fold_in(keys[7], 71), 0)
    fresh_v = centred(keys[2], (TOKENS, HEADS * HD), 1.0, 6.0, ((0, 256),))
    stale_k = draw_stale_k(jax.random.fold_in(keys[7], 71), 0)
    stale_v = centred(keys[4], (TOKENS, HEADS * HD), 1.0, 6.0, ((0, 32), (1, 8)))
    q_gain = jnp.clip(1.0 + 0.18 * jax.random.normal(keys[5], (HEADS * HD,), jnp.float32), 0.1, 1.9)
    k_gain = jnp.clip(1.0 + 0.18 * jax.random.normal(keys[6], (HEADS * HD,), jnp.float32), 0.1, 1.9)
    return dict(fresh_q=fresh_q, fresh_k=fresh_k, fresh_v=fresh_v, stale_k=stale_k, stale_v=stale_v, q_gain=q_gain, k_gain=k_gain)


EPSILON = 1e-06

def rms_rows(source, gain):
    values = source.astype(jnp.float32)
    mean_square = lax.optimization_barrier(jnp.mean(values * values, axis=1, keepdims=True))
    return (values * lax.rsqrt(mean_square + EPSILON) * gain.astype(jnp.float32)[None, :]).astype(jnp.bfloat16)

def reference(fresh_q, fresh_k, fresh_v, stale_k, stale_v, q_gain, k_gain):
    normed_q = rms_rows(fresh_q, q_gain)
    key_cache = rms_rows(fresh_k, k_gain)
    score_scale = HD ** (-0.5)

    def one_patch(patch_index):
        first_row = (patch_index * TOK_PATCH).astype(jnp.int32)
        queries = lax.dynamic_slice_in_dim(normed_q, first_row, TOK_PATCH, 0)
        own_keys = lax.dynamic_slice_in_dim(key_cache, first_row, TOK_PATCH, 0)
        own_values = lax.dynamic_slice_in_dim(fresh_v, first_row, TOK_PATCH, 0)
        key_rows = lax.dynamic_update_slice_in_dim(stale_k, own_keys, first_row, 0)
        value_rows = lax.dynamic_update_slice_in_dim(stale_v, own_values, first_row, 0)

        def one_head(head_index):
            first_col = (head_index * HD).astype(jnp.int32)
            query_head = lax.dynamic_slice_in_dim(queries, first_col, HD, 1)
            key_head = lax.dynamic_slice_in_dim(key_rows, first_col, HD, 1)
            value_head = lax.dynamic_slice_in_dim(value_rows, first_col, HD, 1)
            scores = jnp.dot(query_head, key_head.T, preferred_element_type=jnp.float32) * score_scale
            row_max = lax.optimization_barrier(jnp.max(scores, axis=1, keepdims=True))
            weights = jnp.exp(scores - row_max)
            row_sum = lax.optimization_barrier(jnp.sum(weights, axis=1, keepdims=True))
            mixed = jnp.dot(weights.astype(jnp.bfloat16), value_head, preferred_element_type=jnp.float32)
            return (mixed / row_sum).astype(jnp.bfloat16)
        per_head = lax.map(one_head, jnp.arange(HEADS, dtype=jnp.int32))
        return jnp.transpose(per_head, (1, 0, 2)).reshape(TOK_PATCH, HEADS * HD)
    attended = lax.map(one_patch, jnp.arange(N_PATCH, dtype=jnp.int32))
    return (attended.reshape(TOKENS, HEADS * HD), key_cache)
```

```python
import functools
import jax
import jax.numpy as jnp
from jax import lax
from jax.experimental import pallas as pl
from jax.experimental.pallas import tpu as pltpu
from jax.sharding import Mesh, PartitionSpec as P

HEADS = 24
HD = 128
EPSILON = 1e-06
LOG2E = 1.4426950408889634
SCALE2 = HD**-0.5 * LOG2E
BF = jnp.bfloat16
F32 = jnp.float32
LIMIT = 48 * 2**20
ROWS = 64


def prep_kernel(groups, copies, q_ref, k_ref, v_ref, gq_ref, gk_ref, q_out, kv_out):
    width = q_ref.shape[1]
    per = width // groups

    def norm(src, gain):
        values = src[...].astype(F32)
        mean = jnp.sum(values * values, axis=1, keepdims=True) / width
        return (values * lax.rsqrt(mean + EPSILON) * gain[...]).astype(BF)

    q = norm(q_ref, gq_ref)
    k = norm(k_ref, gk_ref)
    for g in range(groups):
        cols = slice(g * per, (g + 1) * per)
        for c in range(copies):
            q_out[c * groups + g] = q[:, cols]
        kv_out[g, :, :per] = k[:, cols]
        kv_out[g, :, per:] = v_ref[:, cols]


def prep(fresh_q, fresh_k, fresh_v, q_gain, k_gain, groups, copies):
    rows, width = fresh_q.shape
    per = width // groups
    return pl.pallas_call(
        functools.partial(prep_kernel, groups, copies),
        out_shape=(
            jax.ShapeDtypeStruct((copies * groups, rows, per), BF),
            jax.ShapeDtypeStruct((groups, rows, 2 * per), BF),
        ),
        in_specs=[pl.BlockSpec(memory_space=pltpu.VMEM)] * 5,
        out_specs=[pl.BlockSpec(memory_space=pltpu.VMEM)] * 2,
        compiler_params=pltpu.CompilerParams(vmem_limit_bytes=LIMIT),
        name="prep",
    )(fresh_q, fresh_k, fresh_v, q_gain[None, :], k_gain[None, :])


def attn_kernel(nb, fresh, first, last, bq, *refs):
    refs = list(refs)
    own_ref = refs.pop(0) if fresh else None
    q_ref = refs.pop(0)
    k_refs = [refs.pop(0) for _ in range(nb)]
    v_refs = [refs.pop(0) for _ in range(nb)]
    if fresh:
        fk_ref, fv_ref = refs.pop(0), refs.pop(0)
    if not first:
        acc_in, m_in, l_in = refs.pop(0), refs.pop(0), refs.pop(0)
    if last:
        out_ref = refs.pop(0)
    else:
        acc_out, m_out, l_out = refs.pop(0), refs.pop(0), refs.pop(0)
    ks, vs = refs
    head = pl.program_id(0)
    off = 0
    for kr, vr in zip(k_refs, v_refs):
        n = kr.shape[0]
        ks[off : off + n] = kr[...]
        vs[off : off + n, :HD] = vr[...]
        off += n

    @pl.when(head == 0)
    def _():
        vs[:, HD:] = jnp.ones((off, HD), BF)

    nq = q_ref.shape[0]
    tiles = nq // bq

    def scores(t):
        return lax.dot_general(
            q_ref[t * bq : (t + 1) * bq], ks[...], (((1,), (1,)), ((), ())), preferred_element_type=F32
        )

    def rest(t, s):
        rows = slice(t * bq, (t + 1) * bq)
        m = jnp.max(s, axis=1, keepdims=True)
        if not first:
            m_old = m_in[0, rows]
            m = jnp.maximum(m_old[:, :1], m)
        p = jnp.exp2(s * SCALE2 - m * SCALE2).astype(BF)
        o = jnp.dot(p, vs[...], preferred_element_type=F32)
        acc, l = o[:, :HD], o[:, HD:]
        m = jnp.broadcast_to(m, (bq, HD))
        if not first:
            alpha = jnp.exp2((m_old - m) * SCALE2)
            acc = acc + acc_in[0, rows] * alpha
            l = l + l_in[0, rows] * alpha
        if not last:
            acc_out[0, rows], m_out[0, rows], l_out[0, rows] = acc, m, l
            return
        o = (acc / l).astype(BF)
        lse = m * SCALE2 + jnp.log(l) * LOG2E
        tok = ROWS - 16
        eye = lax.broadcasted_iota(jnp.int32, (tok, HD), 0) == lax.broadcasted_iota(jnp.int32, (tok, HD), 1)
        for i in range(bq // tok):
            d = t * (bq // tok) + i
            out_ref[d, :tok] = o[i * tok : (i + 1) * tok]
            row = jnp.sum(jnp.where(eye, lse[i * tok : (i + 1) * tok], 0.0), axis=0, keepdims=True)
            hi = row.astype(BF).astype(F32)
            mid = (row - hi).astype(BF).astype(F32)
            low = row - hi - mid
            which = lax.broadcasted_iota(jnp.int32, (16, HD), 0)
            packed = jnp.where(which == 0, hi, jnp.where(which == 1, mid, jnp.where(which == 2, low, 0.0)))
            out_ref[d, tok:] = packed.astype(BF)

    def run(sweep):
        s = scores(sweep[0])
        for i, t in enumerate(sweep):
            ahead = scores(sweep[i + 1]) if i + 1 < len(sweep) else None
            rest(t, s)
            s = ahead

    if not fresh:
        run(range(tiles))
        return
    n0 = k_refs[0].shape[0]
    patches = nq // n0
    per = tiles // patches
    for j in range(patches):
        own = own_ref[0] == j
        ks[:n0] = jnp.where(own, fk_ref[...], k_refs[0][...])
        vs[:n0, :HD] = jnp.where(own, fv_ref[...], v_refs[0][...])
        run(range(j * per, (j + 1) * per))


def attend(q, blocks, state=None, fresh=None, own=None, last=False, bq=256, name="attend"):
    nq, width = q.shape
    heads = width // HD
    nb = len(blocks)
    keys = sum(b.shape[0] for b in blocks)
    kspec = [pl.BlockSpec((b.shape[0], HD), lambda h: (0, h)) for b in blocks]
    vspec = [pl.BlockSpec((b.shape[0], HD), lambda h: (0, heads + h)) for b in blocks]
    state_spec = pl.BlockSpec((1, nq, HD), lambda h: (h, 0, 0))
    args, specs = [], []
    if fresh is not None:
        args.append(own)
        specs.append(pl.BlockSpec(memory_space=pltpu.SMEM))
    args += [q, *blocks, *blocks]
    specs += [pl.BlockSpec((nq, HD), lambda h: (0, h)), *kspec, *vspec]
    if fresh is not None:
        args += [fresh, fresh]
        n0 = fresh.shape[0]
        specs += [pl.BlockSpec((n0, HD), lambda h: (0, h)), pl.BlockSpec((n0, HD), lambda h: (0, heads + h))]
    if state is not None:
        args += list(state)
        specs += [state_spec] * 3
    if last:
        out_shape = jax.ShapeDtypeStruct((nq // (ROWS - 16), ROWS, width), BF)
        out_specs = pl.BlockSpec((nq // (ROWS - 16), ROWS, HD), lambda h: (0, 0, h))
    else:
        out_shape = [jax.ShapeDtypeStruct((heads, nq, HD), F32)] * 3
        out_specs = [state_spec] * 3
    flops = 4 * nq * keys * width
    return pl.pallas_call(
        functools.partial(attn_kernel, nb, fresh is not None, state is None, last, bq),
        grid=(heads,),
        in_specs=specs,
        out_specs=out_specs,
        out_shape=out_shape,
        scratch_shapes=[pltpu.VMEM((keys, HD), BF), pltpu.VMEM((keys, 2 * HD), BF)],
        compiler_params=pltpu.CompilerParams(vmem_limit_bytes=LIMIT),
        cost_estimate=pl.CostEstimate(flops=flops, bytes_accessed=8 * 2**20, transcendentals=nq * keys * heads),
        name=name,
    )(*args)


def merge_kernel(groups, copies, in_ref, out_ref):
    tok = ROWS - 16
    heads = in_ref.shape[2] // HD
    eye = lax.broadcasted_iota(jnp.int32, (tok, HD), 0) == lax.broadcasted_iota(jnp.int32, (tok, HD), 1)
    for g in range(groups):
        for h in range(heads):
            cols = slice(h * HD, (h + 1) * HD)
            lses = []
            for c in range(copies):
                packed = in_ref[c * groups + g, tok:, cols].astype(F32)
                row = jnp.sum(packed, axis=0, keepdims=True)
                lses.append(jnp.sum(jnp.where(eye, jnp.broadcast_to(row, (tok, HD)), 0.0), axis=1, keepdims=True))
            top = functools.reduce(jnp.maximum, lses)
            weights = [jnp.exp2(x - top) for x in lses]
            total = sum(weights)
            acc = 0.0
            for c in range(copies):
                acc = acc + in_ref[c * groups + g, :tok, cols].astype(F32) * (weights[c] / total)
            first = (g * heads + h) * HD
            out_ref[:, first : first + HD] = acc.astype(BF)


def merge(parts, groups, copies):
    width = parts.shape[2] * groups
    return pl.pallas_call(
        functools.partial(merge_kernel, groups, copies),
        out_shape=jax.ShapeDtypeStruct((ROWS - 16, width), BF),
        in_specs=[pl.BlockSpec(memory_space=pltpu.VMEM)],
        out_specs=pl.BlockSpec(memory_space=pltpu.VMEM),
        compiler_params=pltpu.CompilerParams(vmem_limit_bytes=LIMIT),
        name="merge",
    )(parts)


Z, YL, CORE, X, YH = 8, 2, 2, 4, 2
UP = [(i, (i + 1) % Z) for i in range(Z)]
DOWN = [(i, (i - 1) % Z) for i in range(Z)]
SWAP = [(0, 1), (1, 0)]


def other_core(x):
    return lax.ppermute(x, "core", SWAP)


def body(fresh_q, fresh_k, fresh_v, stale_k, stale_v, q_gain, k_gain):
    groups = X * YH
    width_dev = stale_k.shape[1]
    payload = jnp.concatenate([stale_k, stale_v], axis=1)
    q_parts, kv_parts = prep(fresh_q, fresh_k, fresh_v, q_gain, k_gain, groups, YL)

    up1, down1 = lax.ppermute(payload, "z", UP), lax.ppermute(payload, "z", DOWN)
    q = lax.all_to_all(q_parts, ("yl", "x", "yh"), split_axis=0, concat_axis=0, tiled=True)
    q = q.reshape(-1, width_dev)
    fresh = lax.all_to_all(kv_parts, ("x", "yh"), split_axis=0, concat_axis=0, tiled=True)
    fresh = fresh.reshape(-1, 2 * width_dev)
    own = [payload, other_core(payload)]
    up2, down2 = lax.ppermute(up1, "z", UP), lax.ppermute(down1, "z", DOWN)
    r1 = [up1, down1, other_core(up1), other_core(down1)]
    up3, down3 = lax.ppermute(up2, "z", UP), lax.ppermute(down2, "z", DOWN)
    r2 = [up2, down2, other_core(up2), other_core(down2)]
    half = payload.shape[0] // 2
    up4, down4 = lax.ppermute(up3[:half], "z", UP), lax.ppermute(down3[half:], "z", DOWN)
    r3 = [up3, down3, other_core(up3), other_core(down3)]
    r4 = [up4, down4, other_core(up4), other_core(down4)]

    mine = lax.axis_index("yl").astype(jnp.int32).reshape(1)
    state = attend(q, r1, name="attend1")
    state = attend(q, own + r2, state, fresh=fresh, own=mine, bq=192, name="attend2")
    state = attend(q, r3, state, name="attend3")
    parts = attend(q, r4, state, last=True, bq=384, name="attend4")
    back = lax.all_to_all(parts, ("yl", "x", "yh"), split_axis=0, concat_axis=0, tiled=True)
    return merge(back, groups, YL), fresh[:, :width_dev]


def solution(mesh):
    fine = Mesh(mesh.devices.reshape(Z, YL, CORE, X, YH), ("z", "yl", "core", "x", "yh"))
    patch, head = ("z", "yl", "core"), ("x", "yh")
    tokens = P(patch + head, None)
    tiles = P(patch, head)
    return jax.shard_map(
        body,
        mesh=fine,
        in_specs=(tokens, tokens, tokens, tiles, tiles, P(), P()),
        out_specs=(tokens, tiles),
        check_vma=False,
    )
```

```python
import functools
import jax
import jax.numpy as jnp
from jax import lax
from jax.experimental import pallas as pl
from jax.experimental.pallas import tpu as pltpu
from jax.sharding import Mesh, PartitionSpec as P

HEADS = 24
HD = 128
EPSILON = 1e-06
LOG2E = 1.4426950408889634
SCALE2 = HD**-0.5 * LOG2E
BF = jnp.bfloat16
F32 = jnp.float32
LIMIT = 32 * 2**20
SMALL = 16 * 2**20
ROWS = 64


def norm(src, gain):
    values = src[...].astype(F32)
    mean = jnp.sum(values * values, axis=1, keepdims=True) / src.shape[1]
    return (values * lax.rsqrt(mean + EPSILON) * gain[...]).astype(BF)


def prep_q_kernel(groups, q_ref, gain_ref, out_ref):
    per = q_ref.shape[1] // groups
    q = norm(q_ref, gain_ref)
    for g in range(groups):
        out_ref[g] = q[:, g * per : (g + 1) * per]


def prep_kv_kernel(groups, k_ref, v_ref, gain_ref, out_ref):
    per = k_ref.shape[1] // groups
    k = norm(k_ref, gain_ref)
    for g in range(groups):
        cols = slice(g * per, (g + 1) * per)
        out_ref[g, :, :per] = k[:, cols]
        out_ref[g, :, per:] = v_ref[:, cols]


def prep(kernel, name, groups, gain, *sources):
    rows, width = sources[0].shape
    vmem = pl.BlockSpec(memory_space=pltpu.VMEM)
    return pl.pallas_call(
        functools.partial(kernel, groups),
        out_shape=jax.ShapeDtypeStruct((groups, rows, len(sources) * width // groups), BF),
        in_specs=[vmem] * (len(sources) + 1),
        out_specs=vmem,
        compiler_params=pltpu.CompilerParams(vmem_limit_bytes=SMALL),
        name=name,
    )(*sources, gain[None, :])


def attn_kernel(keys, spans, first, last, *refs):
    refs = list(refs)
    patches = len(spans)
    q_refs = [refs.pop(0) for _ in spans]
    blocks = [refs.pop(0) for _ in keys]
    states = [None if new else (refs.pop(0), refs.pop(0)) for new in first]
    if last:
        base_ref = refs.pop(0)
        out_ref = refs.pop(0)
    else:
        results = [(refs.pop(0), refs.pop(0)) for _ in spans]
    q_buf, k_buf, v_buf, o_buf, lse_buf, sems, out_sem = refs
    nq, width = q_buf.shape
    heads = width // HD
    bq = nq // patches
    total = sum(keys)

    def start(src, dst, sem):
        copy = pltpu.make_async_copy(src, dst, sem)
        copy.start()
        return copy

    early, late = [], []
    off = 0
    for n, block in zip(keys, blocks):
        early.append(start(block.at[:, pl.ds(0, width)], k_buf.at[pl.ds(off, n)], sems.at[0]))
        off += n
    for i, ref in enumerate(q_refs):
        early.append(start(ref, q_buf.at[pl.ds(i * bq, bq)], sems.at[1]))
    off = 0
    for n, block in zip(keys, blocks):
        for h in range(heads):
            src = block.at[:, pl.ds(width + h * HD, HD)]
            late.append(start(src, v_buf.at[h, pl.ds(off, n), pl.ds(0, HD)], sems.at[2]))
        off += n
    for i, state in enumerate(states):
        if state is not None:
            rows = pl.ds(i * bq, bq)
            late.append(start(state[0], o_buf.at[rows], sems.at[3]))
            late.append(start(state[1], lse_buf.at[rows], sems.at[4]))
    for h in range(heads):
        v_buf[h, :, HD:] = jnp.ones((total, HD), BF)
    for copy in early:
        copy.wait()

    def window(i):
        return slice(sum(keys[: spans[i][0]]), sum(keys[: spans[i][1]]))

    def scores(work):
        h, i = work
        cols = slice(h * HD, (h + 1) * HD)
        q = q_buf[i * bq : (i + 1) * bq, cols]
        return lax.dot_general(q, k_buf[window(i), cols], (((1,), (1,)), ((), ())), preferred_element_type=F32)

    tok = ROWS - 16
    lane = lax.broadcasted_iota(jnp.int32, (bq, HD), 1)
    eye = lax.broadcasted_iota(jnp.int32, (tok, HD), 0) == lax.broadcasted_iota(jnp.int32, (tok, HD), 1)
    which = lax.broadcasted_iota(jnp.int32, (16, HD), 0)
    done = [None] * patches

    def rest(work, s):
        h, i = work
        rows, cols = slice(i * bq, (i + 1) * bq), slice(h * HD, (h + 1) * HD)
        m = jnp.max(s, axis=1, keepdims=True) * SCALE2
        if not first[i]:
            lse_old = lse_buf[rows][:, h : h + 1]
            m = jnp.maximum(lse_old, m)
        p = jnp.exp2(s * SCALE2 - m).astype(BF)
        o = jnp.dot(p, v_buf[h, window(i)], preferred_element_type=F32)
        a, l = o[:, :HD], o[:, HD:]
        if not first[i]:
            old = jnp.exp2(lse_old - m)
            a = a + o_buf[rows, cols].astype(F32) * old
            l = l + old
        o = (a / l).astype(BF)
        lse = m + jnp.log(l) * LOG2E
        if not last:
            o_buf[rows, cols] = o
            done[i] = lse if h == 0 else jnp.where(lane == h, lse, done[i])
            if h == heads - 1:
                lse_buf[rows] = done[i]
            return
        for t in range(bq // tok):
            d = base_ref[i] + t
            out_ref[d, :tok, cols] = o[t * tok : (t + 1) * tok]
            row = jnp.sum(jnp.where(eye, lse[t * tok : (t + 1) * tok], 0.0), axis=0, keepdims=True)
            hi = row.astype(BF).astype(F32)
            mid = (row - hi).astype(BF).astype(F32)
            low = row - hi - mid
            packed = jnp.where(which == 0, hi, jnp.where(which == 1, mid, jnp.where(which == 2, low, 0.0)))
            out_ref[d, tok:, cols] = packed.astype(BF)

    pending = None
    for work in [(h, i) for h in range(heads) for i in range(patches)]:
        s = scores(work)
        if pending is None:
            for copy in late:
                copy.wait()
        else:
            rest(*pending)
        pending = (work, s)
    rest(*pending)
    if not last:
        stores = []
        for i, (o_hbm, lse_hbm) in enumerate(results):
            rows = pl.ds(i * bq, bq)
            stores.append(start(o_buf.at[rows], o_hbm, out_sem.at[0]))
            stores.append(start(lse_buf.at[rows], lse_hbm, out_sem.at[1]))
        for copy in stores:
            copy.wait()


def attend(qs, blocks, states=None, spans=None, base=None, name="attend"):
    bq, width = qs[0].shape
    patches = len(qs)
    nq = patches * bq
    heads = width // HD
    keys = tuple(b.shape[0] for b in blocks)
    states = states or [None] * patches
    spans = spans or [(0, len(keys))] * patches
    first, last = [s is None for s in states], base is not None
    total = sum(keys)
    hbm = pl.BlockSpec(memory_space=pl.ANY)
    args = [*qs, *blocks]
    alias = {}
    for i, state in enumerate(states):
        if state is not None:
            if not last:
                alias |= {len(args): 2 * i, len(args) + 1: 2 * i + 1}
            args += list(state)
    specs = [hbm] * len(args)
    if last:
        args.append(base)
        specs.append(pl.BlockSpec(memory_space=pltpu.SMEM))
        out_shape = jax.ShapeDtypeStruct((nq // (ROWS - 16), ROWS, width), BF)
        out_specs = pl.BlockSpec(memory_space=pltpu.VMEM)
    else:
        out_shape = [jax.ShapeDtypeStruct((bq, width), BF), jax.ShapeDtypeStruct((bq, HD), F32)] * patches
        out_specs = [hbm] * len(out_shape)
    seen = sum(sum(keys[a:b]) for a, b in spans)
    out = pl.pallas_call(
        functools.partial(attn_kernel, keys, spans, first, last),
        in_specs=specs,
        out_specs=out_specs,
        out_shape=out_shape,
        scratch_shapes=[
            pltpu.VMEM((nq, width), BF),
            pltpu.VMEM((total, width), BF),
            pltpu.VMEM((heads, total, 2 * HD), BF),
            pltpu.VMEM((nq, width), BF),
            pltpu.VMEM((nq, HD), F32),
            pltpu.SemaphoreType.DMA((5,)),
            pltpu.SemaphoreType.DMA((2,)),
        ],
        input_output_aliases=alias,
        compiler_params=pltpu.CompilerParams(vmem_limit_bytes=LIMIT),
        cost_estimate=pl.CostEstimate(flops=4 * bq * seen * width, bytes_accessed=2**20, transcendentals=bq * seen * heads),
        name=name,
    )(*args)
    return out if last else [out[2 * i : 2 * i + 2] for i in range(patches)]


def merge_kernel(groups, copies, in_ref, out_ref):
    tok = ROWS - 16
    heads = in_ref.shape[2] // HD
    eye = lax.broadcasted_iota(jnp.int32, (tok, HD), 0) == lax.broadcasted_iota(jnp.int32, (tok, HD), 1)
    for g in range(groups):
        for h in range(heads):
            cols = slice(h * HD, (h + 1) * HD)
            lses = []
            for c in range(copies):
                packed = in_ref[c * groups + g, tok:, cols].astype(F32)
                row = jnp.sum(packed, axis=0, keepdims=True)
                lses.append(jnp.sum(jnp.where(eye, jnp.broadcast_to(row, (tok, HD)), 0.0), axis=1, keepdims=True))
            top = functools.reduce(jnp.maximum, lses)
            weights = [jnp.exp2(x - top) for x in lses]
            total = sum(weights)
            acc = 0.0
            for c in range(copies):
                acc = acc + in_ref[c * groups + g, :tok, cols].astype(F32) * (weights[c] / total)
            first = (g * heads + h) * HD
            out_ref[:, first : first + HD] = acc.astype(BF)


def merge(parts, groups, copies):
    width = parts.shape[2] * groups
    return pl.pallas_call(
        functools.partial(merge_kernel, groups, copies),
        out_shape=jax.ShapeDtypeStruct((ROWS - 16, width), BF),
        in_specs=[pl.BlockSpec(memory_space=pltpu.VMEM)],
        out_specs=pl.BlockSpec(memory_space=pltpu.VMEM),
        compiler_params=pltpu.CompilerParams(vmem_limit_bytes=SMALL),
        name="merge",
    )(parts)


Z, YL, CORE, X, YH = 8, 2, 2, 4, 2
UP = [(i, (i + 1) % Z) for i in range(Z)]
DOWN = [(i, (i - 1) % Z) for i in range(Z)]
SWAP = [(0, 1), (1, 0)]


def other_core(x):
    return lax.ppermute(x, "core", SWAP)


def body(fresh_q, fresh_k, fresh_v, stale_k, stale_v, q_gain, k_gain):
    groups = X * YH
    width_dev = stale_k.shape[1]
    half = stale_k.shape[0] // 2
    yl = lax.axis_index("yl").astype(jnp.int32)
    base = jnp.stack([yl * groups, (1 - yl) * groups])

    def both(pair):
        return lax.ppermute(pair[0], "z", UP), lax.ppermute(pair[1], "z", DOWN)

    def swap(pair):
        return other_core(pair[0]), other_core(pair[1])

    own = jnp.concatenate([stale_k, stale_v], axis=1)
    r1 = both((own, own))
    q_parts = prep(prep_q_kernel, "prep_q", groups, q_gain, fresh_q)
    q = lax.all_to_all(q_parts, ("x", "yh"), split_axis=0, concat_axis=0, tiled=True)
    kv_parts = prep(prep_kv_kernel, "prep_kv", groups, k_gain, fresh_k, fresh_v)
    r1, q, kv_parts = lax.optimization_barrier((r1, q, kv_parts))
    q = q.reshape(-1, width_dev)
    qs = [q, lax.ppermute(q, "yl", SWAP)]
    r2 = both(r1)
    fresh = lax.all_to_all(kv_parts, ("x", "yh"), split_axis=0, concat_axis=0, tiled=True)
    own_other = other_core(own)
    r1 = [*r1, *swap(r1)]
    early = attend(qs[:1], [own_other, *r1], name="attend1")
    r2, qs[1], fresh, early = lax.optimization_barrier((r2, qs[1], fresh, early))
    fresh = fresh.reshape(-1, 2 * width_dev)

    r3 = both(r2)
    blocks = [own, own_other, *r1, *r2, *swap(r2), fresh]
    state = attend(qs, blocks, [early[0], None], [(6, 11), (0, 10)], name="attend2")
    r3, state = lax.optimization_barrier((r3, state))
    r4 = both((r3[0][:half], r3[1][half:]))
    state = attend(qs, [*r3, *swap(r3)], state, name="attend3")
    r4, state = lax.optimization_barrier((r4, state))
    parts = attend(qs, [*r4, *swap(r4)], state, base=base, name="attend4")
    back = lax.all_to_all(parts, ("yl", "x", "yh"), split_axis=0, concat_axis=0, tiled=True)
    return merge(back, groups, YL), fresh[:, :width_dev]


def solution(mesh):
    fine = Mesh(mesh.devices.reshape(Z, YL, CORE, X, YH), ("z", "yl", "core", "x", "yh"))
    patch, head = ("z", "yl", "core"), ("x", "yh")
    tokens = P(patch + head, None)
    tiles = P(patch, head)
    return jax.shard_map(
        body,
        mesh=fine,
        in_specs=(tokens, tokens, tokens, tiles, tiles, P(), P()),
        out_specs=(tokens, tiles),
        check_vma=False,
    )
```

```python
import functools
import jax
import jax.numpy as jnp
from jax import lax
from jax.experimental import pallas as pl
from jax.experimental.pallas import tpu as pltpu
from jax.sharding import Mesh, PartitionSpec as P

HEADS = 24
HD = 128
EPSILON = 1e-06
LOG2E = 1.4426950408889634
SCALE2 = HD**-0.5 * LOG2E
BF = jnp.bfloat16
F32 = jnp.float32
LIMIT = 32 * 2**20
SMALL = 16 * 2**20
TOK, EXTRA = 48, 8


def norm(src, gain):
    values = src[...].astype(F32)
    mean = jnp.sum(values * values, axis=1, keepdims=True) / src.shape[1]
    return (values * lax.rsqrt(mean + EPSILON) * gain[...]).astype(BF)


def prep_q_kernel(copies, groups, q_ref, gain_ref, out_ref):
    per = q_ref.shape[1] // groups
    q = norm(q_ref, gain_ref)
    for g in range(groups):
        for c in range(copies):
            out_ref[c * groups + g] = q[:, g * per : (g + 1) * per]


def prep_kv_kernel(copies, groups, k_ref, v_ref, gain_ref, out_ref):
    per = k_ref.shape[1] // groups
    k = norm(k_ref, gain_ref)
    for g in range(groups):
        cols = slice(g * per, (g + 1) * per)
        out_ref[g, :, :per] = k[:, cols]
        out_ref[g, :, per:] = v_ref[:, cols]


def prep(kernel, name, copies, groups, gain, *sources):
    rows, width = sources[0].shape
    vmem = pl.BlockSpec(memory_space=pltpu.VMEM)
    return pl.pallas_call(
        functools.partial(kernel, copies, groups),
        out_shape=jax.ShapeDtypeStruct((copies * groups, rows, len(sources) * width // groups), BF),
        in_specs=[vmem] * (len(sources) + 1),
        out_specs=vmem,
        compiler_params=pltpu.CompilerParams(vmem_limit_bytes=SMALL),
        name=name,
    )(*sources, gain[None, :])


def attn_kernel(keys, spans, first, last, *refs):
    refs = list(refs)
    patches = len(spans)
    q_ref = refs.pop(0)
    blocks = [refs.pop(0) for _ in keys]
    states = [None if new else (refs.pop(0), refs.pop(0)) for new in first]
    yl_ref = refs.pop(0)
    place = [yl_ref[0], 1 - yl_ref[0]]
    if last:
        out_ref = refs.pop(0)
    else:
        results = [(refs.pop(0), refs.pop(0)) for _ in spans]
    q_buf, k_buf, v_buf, o_buf, lse_buf, sems, out_sem = refs
    nq, width = q_buf.shape
    heads = width // HD
    bq = nq // patches
    total = sum(keys)

    def start(src, dst, sem):
        copy = pltpu.make_async_copy(src, dst, sem)
        copy.start()
        return copy

    early, late = [], []
    off = 0
    for n, block in zip(keys, blocks):
        early.append(start(block.at[:, pl.ds(0, width)], k_buf.at[pl.ds(off, n)], sems.at[0]))
        off += n
    for i in range(patches):
        src = q_ref.at[pl.ds(pl.multiple_of(place[i] * bq, bq), bq)]
        early.append(start(src, q_buf.at[pl.ds(i * bq, bq)], sems.at[1]))
    off = 0
    for n, block in zip(keys, blocks):
        for h in range(heads):
            src = block.at[:, pl.ds(width + h * HD, HD)]
            late.append(start(src, v_buf.at[h, pl.ds(off, n), pl.ds(0, HD)], sems.at[2]))
        off += n
    for i, state in enumerate(states):
        if state is not None:
            rows = pl.ds(i * bq, bq)
            late.append(start(state[0], o_buf.at[rows], sems.at[3]))
            late.append(start(state[1], lse_buf.at[rows], sems.at[4]))
    for h in range(heads):
        v_buf[h, :, HD:] = jnp.ones((total, HD), BF)
    for copy in early:
        copy.wait()

    def window(i):
        return slice(sum(keys[: spans[i][0]]), sum(keys[: spans[i][1]]))

    def scores(work):
        h, i = work
        cols = slice(h * HD, (h + 1) * HD)
        q = q_buf[i * bq : (i + 1) * bq, cols]
        return lax.dot_general(q, k_buf[window(i), cols], (((1,), (1,)), ((), ())), preferred_element_type=F32)

    tok = TOK
    lane = lax.broadcasted_iota(jnp.int32, (bq, HD), 1)
    eye = lax.broadcasted_iota(jnp.int32, (tok, HD), 0) == lax.broadcasted_iota(jnp.int32, (tok, HD), 1)
    which = lax.broadcasted_iota(jnp.int32, (EXTRA, HD), 0)
    done = [None] * patches

    def rest(work, s):
        h, i = work
        rows, cols = slice(i * bq, (i + 1) * bq), slice(h * HD, (h + 1) * HD)
        m = jnp.max(s, axis=1, keepdims=True) * SCALE2
        if not first[i]:
            lse_old = lse_buf[rows][:, h : h + 1]
            m = jnp.maximum(lse_old, m)
        p = jnp.exp2(s * SCALE2 - m).astype(BF)
        o = jnp.dot(p, v_buf[h, window(i)], preferred_element_type=F32)
        a, l = o[:, :HD], o[:, HD:]
        if not first[i]:
            old = jnp.exp2(lse_old - m)
            a = a + o_buf[rows, cols].astype(F32) * old
            l = l + old
        o = (a / l).astype(BF)
        lse = m + jnp.log(l) * LOG2E
        if not last:
            o_buf[rows, cols] = o
            done[i] = lse if h == 0 else jnp.where(lane == h, lse, done[i])
            if h == heads - 1:
                lse_buf[rows] = done[i]
            return
        for t in range(bq // tok):
            d = place[i] * (bq // tok) + t
            row = jnp.sum(jnp.where(eye, lse[t * tok : (t + 1) * tok], 0.0), axis=0, keepdims=True)
            hi = row.astype(BF).astype(F32)
            mid = (row - hi).astype(BF).astype(F32)
            low = row - hi - mid
            packed = jnp.where(which == 0, hi, jnp.where(which == 1, mid, jnp.where(which == 2, low, 0.0)))
            out_ref[d, :, cols] = jnp.concatenate([o[t * tok : (t + 1) * tok], packed.astype(BF)], axis=0)

    pending = None
    for work in [(h, i) for h in range(heads) for i in range(patches)]:
        s = scores(work)
        if pending is None:
            for copy in late:
                copy.wait()
        else:
            rest(*pending)
        pending = (work, s)
    rest(*pending)
    if not last:
        stores = []
        for i, (o_hbm, lse_hbm) in enumerate(results):
            rows = pl.ds(i * bq, bq)
            stores.append(start(o_buf.at[rows], o_hbm, out_sem.at[0]))
            stores.append(start(lse_buf.at[rows], lse_hbm, out_sem.at[1]))
        for copy in stores:
            copy.wait()


def attend(q, yl, blocks, states=None, spans=None, last=False, name="attend"):
    nq, width = q.shape
    patches = YL
    bq = nq // patches
    heads = width // HD
    keys = tuple(b.shape[0] for b in blocks)
    states = states or [None] * patches
    spans = spans or [(0, len(keys))] * patches
    first = [s is None for s in states]
    total = sum(keys)
    hbm = pl.BlockSpec(memory_space=pl.ANY)
    args = [q, *blocks]
    alias = {}
    for i, state in enumerate(states):
        if state is not None:
            if not last:
                alias |= {len(args): 2 * i, len(args) + 1: 2 * i + 1}
            args += list(state)
    args.append(yl)
    specs = [hbm] * (len(args) - 1) + [pl.BlockSpec(memory_space=pltpu.SMEM)]
    if last:
        out_shape = jax.ShapeDtypeStruct((nq // TOK, TOK + EXTRA, width), BF)
        out_specs = pl.BlockSpec(memory_space=pltpu.VMEM)
    else:
        out_shape = [jax.ShapeDtypeStruct((bq, width), BF), jax.ShapeDtypeStruct((bq, HD), F32)] * patches
        out_specs = [hbm] * len(out_shape)
    seen = sum(sum(keys[a:b]) for a, b in spans)
    out = pl.pallas_call(
        functools.partial(attn_kernel, keys, spans, first, last),
        in_specs=specs,
        out_specs=out_specs,
        out_shape=out_shape,
        scratch_shapes=[
            pltpu.VMEM((nq, width), BF),
            pltpu.VMEM((total, width), BF),
            pltpu.VMEM((heads, total, 2 * HD), BF),
            pltpu.VMEM((nq, width), BF),
            pltpu.VMEM((nq, HD), F32),
            pltpu.SemaphoreType.DMA((5,)),
            pltpu.SemaphoreType.DMA((2,)),
        ],
        input_output_aliases=alias,
        compiler_params=pltpu.CompilerParams(vmem_limit_bytes=LIMIT),
        cost_estimate=pl.CostEstimate(flops=4 * bq * seen * width, bytes_accessed=2**20, transcendentals=bq * seen * heads),
        name=name,
    )(*args)
    return out if last else [out[2 * i : 2 * i + 2] for i in range(patches)]


def merge_kernel(groups, copies, in_ref, out_ref):
    tok = TOK
    heads = in_ref.shape[2] // HD
    eye = lax.broadcasted_iota(jnp.int32, (tok, HD), 0) == lax.broadcasted_iota(jnp.int32, (tok, HD), 1)
    for g in range(groups):
        for h in range(heads):
            cols = slice(h * HD, (h + 1) * HD)
            parts = [in_ref[c * groups + g, :, cols].astype(F32) for c in range(copies)]
            lses = []
            for part in parts:
                row = jnp.sum(part[tok:], axis=0, keepdims=True)
                lses.append(jnp.sum(jnp.where(eye, jnp.broadcast_to(row, (tok, HD)), 0.0), axis=1, keepdims=True))
            top = functools.reduce(jnp.maximum, lses)
            weights = [jnp.exp2(x - top) for x in lses]
            total = sum(weights)
            acc = sum(part[:tok] * (weight / total) for part, weight in zip(parts, weights))
            first = (g * heads + h) * HD
            out_ref[:, first : first + HD] = acc.astype(BF)


def merge(parts, groups, copies):
    width = parts.shape[2] * groups
    return pl.pallas_call(
        functools.partial(merge_kernel, groups, copies),
        out_shape=jax.ShapeDtypeStruct((TOK, width), BF),
        in_specs=[pl.BlockSpec(memory_space=pltpu.VMEM)],
        out_specs=pl.BlockSpec(memory_space=pltpu.VMEM),
        compiler_params=pltpu.CompilerParams(vmem_limit_bytes=SMALL),
        name="merge",
    )(parts)


Z, YL, CORE, X, YH = 8, 2, 2, 4, 2
UP = [(i, (i + 1) % Z) for i in range(Z)]
DOWN = [(i, (i - 1) % Z) for i in range(Z)]
SWAP = [(0, 1), (1, 0)]


def other_core(x):
    return lax.ppermute(x, "core", SWAP)


def body(fresh_q, fresh_k, fresh_v, stale_k, stale_v, q_gain, k_gain):
    groups = X * YH
    width_dev = stale_k.shape[1]
    half = stale_k.shape[0] // 2
    yl = lax.axis_index("yl").astype(jnp.int32).reshape(1)

    def both(pair):
        return lax.ppermute(pair[0], "z", UP), lax.ppermute(pair[1], "z", DOWN)

    def swap(pair):
        return other_core(pair[0]), other_core(pair[1])

    own = jnp.concatenate([stale_k, stale_v], axis=1)
    r1 = both((own, own))
    q_parts = prep(prep_q_kernel, "prep_q", YL, groups, q_gain, fresh_q)
    q = lax.all_to_all(q_parts, ("yl", "x", "yh"), split_axis=0, concat_axis=0, tiled=True)
    kv_parts = prep(prep_kv_kernel, "prep_kv", 1, groups, k_gain, fresh_k, fresh_v)
    r1, q, kv_parts = lax.optimization_barrier((r1, q, kv_parts))
    q = q.reshape(-1, width_dev)
    r2 = both(r1)
    fresh = lax.all_to_all(kv_parts, ("x", "yh"), split_axis=0, concat_axis=0, tiled=True)
    own_other = other_core(own)
    state = attend(q, yl, [*r1, *swap(r1)], name="attend1")
    r2, state, fresh = lax.optimization_barrier((r2, state, fresh))
    fresh = fresh.reshape(-1, 2 * width_dev)

    r3 = both(r2)
    blocks = [own, own_other, *r2, *swap(r2), fresh]
    state = attend(q, yl, blocks, state, [(1, 7), (0, 6)], name="attend2")
    r3, state = lax.optimization_barrier((r3, state))
    r4 = both((r3[0][:half], r3[1][half:]))
    state = attend(q, yl, [*r3, *swap(r3)], state, name="attend3")
    r4, state = lax.optimization_barrier((r4, state))
    parts = attend(q, yl, [*r4, *swap(r4)], state, last=True, name="attend4")
    back = lax.all_to_all(parts, ("yl", "x", "yh"), split_axis=0, concat_axis=0, tiled=True)
    return merge(back, groups, YL), fresh[:, :width_dev]


def solution(mesh):
    fine = Mesh(mesh.devices.reshape(Z, YL, CORE, X, YH), ("z", "yl", "core", "x", "yh"))
    patch, head = ("z", "yl", "core"), ("x", "yh")
    tokens = P(patch + head, None)
    tiles = P(patch, head)
    return jax.shard_map(
        body,
        mesh=fine,
        in_specs=(tokens, tokens, tokens, tiles, tiles, P(), P()),
        out_specs=(tokens, tiles),
        check_vma=False,
    )
```

```python
import functools
import jax
import jax.numpy as jnp
from jax import lax
from jax.experimental import pallas as pl
from jax.experimental.pallas import tpu as pltpu
from jax.sharding import Mesh, PartitionSpec as P

HEADS = 24
HD = 128
EPSILON = 1e-06
LOG2E = 1.4426950408889634
SCALE2 = HD**-0.5 * LOG2E
BF = jnp.bfloat16
F32 = jnp.float32
LIMIT = 32 * 2**20
SMALL = 16 * 2**20
TOK, EXTRA = 48, 8


def norm(src, gain):
    values = src[...].astype(F32)
    mean = jnp.sum(values * values, axis=1, keepdims=True) / src.shape[1]
    return (values * lax.rsqrt(mean + EPSILON) * gain[...]).astype(BF)


def prep_q_kernel(copies, groups, q_ref, gain_ref, out_ref):
    per = q_ref.shape[1] // groups
    q = norm(q_ref, gain_ref)
    for g in range(groups):
        for c in range(copies):
            out_ref[c * groups + g] = q[:, g * per : (g + 1) * per]


def prep_kv_kernel(copies, groups, k_ref, v_ref, gain_ref, out_ref):
    per = k_ref.shape[1] // groups
    k = norm(k_ref, gain_ref)
    for g in range(groups):
        cols = slice(g * per, (g + 1) * per)
        out_ref[g, :, :per] = k[:, cols]
        out_ref[g, :, per:] = v_ref[:, cols]


def prep(kernel, name, copies, groups, gain, *sources):
    rows, width = sources[0].shape
    vmem = pl.BlockSpec(memory_space=pltpu.VMEM)
    return pl.pallas_call(
        functools.partial(kernel, copies, groups),
        out_shape=jax.ShapeDtypeStruct((copies * groups, rows, len(sources) * width // groups), BF),
        in_specs=[vmem] * (len(sources) + 1),
        out_specs=vmem,
        compiler_params=pltpu.CompilerParams(vmem_limit_bytes=SMALL),
        name=name,
    )(*sources, gain[None, :])


def attn_kernel(keys, spans, first, last, *refs):
    refs = list(refs)
    patches = len(spans)
    q_ref = refs.pop(0)
    blocks = [refs.pop(0) for _ in keys]
    states = [None if new else (refs.pop(0), refs.pop(0)) for new in first]
    yl_ref = refs.pop(0)
    place = [yl_ref[0], 1 - yl_ref[0]]
    if last:
        out_ref = refs.pop(0)
    else:
        results = [(refs.pop(0), refs.pop(0)) for _ in spans]
    q_buf, k_buf, v_buf, o_buf, lse_buf, sems, out_sem = refs
    nq, width = q_buf.shape
    heads = width // HD
    bq = nq // patches
    total = sum(keys)

    def start(src, dst, sem):
        copy = pltpu.make_async_copy(src, dst, sem)
        copy.start()
        return copy

    early, late = [], []
    off = 0
    for n, block in zip(keys, blocks):
        early.append(start(block.at[:, pl.ds(0, width)], k_buf.at[pl.ds(off, n)], sems.at[0]))
        off += n
    for i in range(patches):
        src = q_ref.at[pl.ds(pl.multiple_of(place[i] * bq, bq), bq)]
        early.append(start(src, q_buf.at[pl.ds(i * bq, bq)], sems.at[1]))
    off = 0
    for n, block in zip(keys, blocks):
        for h in range(heads):
            src = block.at[:, pl.ds(width + h * HD, HD)]
            late.append(start(src, v_buf.at[h, pl.ds(off, n), pl.ds(0, HD)], sems.at[2]))
        off += n
    for i, state in enumerate(states):
        if state is not None:
            rows = pl.ds(i * bq, bq)
            late.append(start(state[0], o_buf.at[rows], sems.at[3]))
            late.append(start(state[1], lse_buf.at[rows], sems.at[4]))
    for h in range(heads):
        v_buf[h, :, HD:] = jnp.ones((total, HD), BF)
    for copy in early:
        copy.wait()

    def window(i):
        return slice(sum(keys[: spans[i][0]]), sum(keys[: spans[i][1]]))

    def scores(work):
        h, i = work
        cols = slice(h * HD, (h + 1) * HD)
        q = q_buf[i * bq : (i + 1) * bq, cols]
        return lax.dot_general(q, k_buf[window(i), cols], (((1,), (1,)), ((), ())), preferred_element_type=F32)

    tok = TOK
    lane = lax.broadcasted_iota(jnp.int32, (bq, HD), 1)
    eye = lax.broadcasted_iota(jnp.int32, (tok, HD), 0) == lax.broadcasted_iota(jnp.int32, (tok, HD), 1)
    which = lax.broadcasted_iota(jnp.int32, (EXTRA, HD), 0)
    done = [None] * patches

    def rest(work, s):
        h, i = work
        rows, cols = slice(i * bq, (i + 1) * bq), slice(h * HD, (h + 1) * HD)
        m = jnp.max(s, axis=1, keepdims=True) * SCALE2
        if not first[i]:
            lse_old = lse_buf[rows][:, h : h + 1]
            m = jnp.maximum(lse_old, m)
        p = jnp.exp2(s * SCALE2 - m).astype(BF)
        o = jnp.dot(p, v_buf[h, window(i)], preferred_element_type=F32)
        a, l = o[:, :HD], o[:, HD:]
        if not first[i]:
            old = jnp.exp2(lse_old - m)
            a = a + o_buf[rows, cols].astype(F32) * old
            l = l + old
        o = (a / l).astype(BF)
        lse = m + jnp.log(l) * LOG2E
        if not last:
            o_buf[rows, cols] = o
            done[i] = lse if h == 0 else jnp.where(lane == h, lse, done[i])
            if h == heads - 1:
                lse_buf[rows] = done[i]
            return
        for t in range(bq // tok):
            d = place[i] * (bq // tok) + t
            row = jnp.sum(jnp.where(eye, lse[t * tok : (t + 1) * tok], 0.0), axis=0, keepdims=True)
            hi = row.astype(BF).astype(F32)
            mid = (row - hi).astype(BF).astype(F32)
            low = row - hi - mid
            packed = jnp.where(which == 0, hi, jnp.where(which == 1, mid, jnp.where(which == 2, low, 0.0)))
            out_ref[d, :, cols] = jnp.concatenate([o[t * tok : (t + 1) * tok], packed.astype(BF)], axis=0)

    pending = None
    for work in [(h, i) for h in range(heads) for i in range(patches)]:
        s = scores(work)
        if pending is None:
            for copy in late:
                copy.wait()
        else:
            rest(*pending)
        pending = (work, s)
    rest(*pending)
    if not last:
        stores = []
        for i, (o_hbm, lse_hbm) in enumerate(results):
            rows = pl.ds(i * bq, bq)
            stores.append(start(o_buf.at[rows], o_hbm, out_sem.at[0]))
            stores.append(start(lse_buf.at[rows], lse_hbm, out_sem.at[1]))
        for copy in stores:
            copy.wait()


def attend(q, yl, blocks, states=None, spans=None, last=False, name="attend"):
    nq, width = q.shape
    patches = YL
    bq = nq // patches
    heads = width // HD
    keys = tuple(b.shape[0] for b in blocks)
    states = states or [None] * patches
    spans = spans or [(0, len(keys))] * patches
    first = [s is None for s in states]
    total = sum(keys)
    hbm = pl.BlockSpec(memory_space=pl.ANY)
    args = [q, *blocks]
    alias = {}
    for i, state in enumerate(states):
        if state is not None:
            if not last:
                alias |= {len(args): 2 * i, len(args) + 1: 2 * i + 1}
            args += list(state)
    args.append(yl)
    specs = [hbm] * (len(args) - 1) + [pl.BlockSpec(memory_space=pltpu.SMEM)]
    if last:
        out_shape = jax.ShapeDtypeStruct((nq // TOK, TOK + EXTRA, width), BF)
        out_specs = pl.BlockSpec(memory_space=pltpu.VMEM)
    else:
        out_shape = [jax.ShapeDtypeStruct((bq, width), BF), jax.ShapeDtypeStruct((bq, HD), F32)] * patches
        out_specs = [hbm] * len(out_shape)
    seen = sum(sum(keys[a:b]) for a, b in spans)
    out = pl.pallas_call(
        functools.partial(attn_kernel, keys, spans, first, last),
        in_specs=specs,
        out_specs=out_specs,
        out_shape=out_shape,
        scratch_shapes=[
            pltpu.VMEM((nq, width), BF),
            pltpu.VMEM((total, width), BF),
            pltpu.VMEM((heads, total, 2 * HD), BF),
            pltpu.VMEM((nq, width), BF),
            pltpu.VMEM((nq, HD), F32),
            pltpu.SemaphoreType.DMA((5,)),
            pltpu.SemaphoreType.DMA((2,)),
        ],
        input_output_aliases=alias,
        compiler_params=pltpu.CompilerParams(vmem_limit_bytes=LIMIT),
        cost_estimate=pl.CostEstimate(flops=4 * bq * seen * width, bytes_accessed=2**20, transcendentals=bq * seen * heads),
        name=name,
    )(*args)
    return out if last else [out[2 * i : 2 * i + 2] for i in range(patches)]


def merge_kernel(groups, copies, in_ref, out_ref):
    tok = TOK
    heads = in_ref.shape[2] // HD
    eye = lax.broadcasted_iota(jnp.int32, (tok, HD), 0) == lax.broadcasted_iota(jnp.int32, (tok, HD), 1)
    for g in range(groups):
        for h in range(heads):
            cols = slice(h * HD, (h + 1) * HD)
            parts = [in_ref[c * groups + g, :, cols].astype(F32) for c in range(copies)]
            lses = []
            for part in parts:
                row = jnp.sum(part[tok:], axis=0, keepdims=True)
                lses.append(jnp.sum(jnp.where(eye, jnp.broadcast_to(row, (tok, HD)), 0.0), axis=1, keepdims=True))
            top = functools.reduce(jnp.maximum, lses)
            weights = [jnp.exp2(x - top) for x in lses]
            total = sum(weights)
            acc = sum(part[:tok] * (weight / total) for part, weight in zip(parts, weights))
            first = (g * heads + h) * HD
            out_ref[:, first : first + HD] = acc.astype(BF)


def merge(parts, groups, copies):
    width = parts.shape[2] * groups
    return pl.pallas_call(
        functools.partial(merge_kernel, groups, copies),
        out_shape=jax.ShapeDtypeStruct((TOK, width), BF),
        in_specs=[pl.BlockSpec(memory_space=pltpu.VMEM)],
        out_specs=pl.BlockSpec(memory_space=pltpu.VMEM),
        compiler_params=pltpu.CompilerParams(vmem_limit_bytes=SMALL),
        name="merge",
    )(parts)


Z, YL, CORE, X, YH = 8, 2, 2, 4, 2
UP = [(i, (i + 1) % Z) for i in range(Z)]
DOWN = [(i, (i - 1) % Z) for i in range(Z)]
SWAP = [(0, 1), (1, 0)]


def other_core(x):
    return lax.ppermute(x, "core", SWAP)


def body(fresh_q, fresh_k, fresh_v, stale_k, stale_v, q_gain, k_gain):
    groups = X * YH
    width_dev = stale_k.shape[1]
    half = stale_k.shape[0] // 2
    yl = lax.axis_index("yl").astype(jnp.int32).reshape(1)

    def both(pair):
        return lax.ppermute(pair[0], "z", UP), lax.ppermute(pair[1], "z", DOWN)

    def swap(pair):
        return other_core(pair[0]), other_core(pair[1])

    own = jnp.concatenate([stale_k, stale_v], axis=1)
    r1 = both((own, own))
    q_parts = prep(prep_q_kernel, "prep_q", YL, groups, q_gain, fresh_q)
    q = lax.all_to_all(q_parts, ("yl", "x", "yh"), split_axis=0, concat_axis=0, tiled=True)
    kv_parts = prep(prep_kv_kernel, "prep_kv", 1, groups, k_gain, fresh_k, fresh_v)
    down1, q, kv_parts = lax.optimization_barrier((r1[1], q, kv_parts))
    r1 = (r1[0], down1)
    q = q.reshape(-1, width_dev)
    r2 = both(r1)
    fresh = lax.all_to_all(kv_parts, ("x", "yh"), split_axis=0, concat_axis=0, tiled=True)
    own_other = other_core(own)
    state = attend(q, yl, [*r1, *swap(r1)], name="attend1")
    r2, state, fresh = lax.optimization_barrier((r2, state, fresh))
    fresh = fresh.reshape(-1, 2 * width_dev)

    r3 = both(r2)
    blocks = [own, own_other, *r2, *swap(r2), fresh]
    state = attend(q, yl, blocks, state, [(1, 7), (0, 6)], name="attend2")
    r3, state = lax.optimization_barrier((r3, state))
    r4 = both((r3[0][:half], r3[1][half:]))
    state = attend(q, yl, [*r3, *swap(r3)], state, name="attend3")
    r4, state = lax.optimization_barrier((r4, state))
    parts = attend(q, yl, [*r4, *swap(r4)], state, last=True, name="attend4")
    back = lax.all_to_all(parts, ("yl", "x", "yh"), split_axis=0, concat_axis=0, tiled=True)
    return merge(back, groups, YL), fresh[:, :width_dev]


def solution(mesh):
    fine = Mesh(mesh.devices.reshape(Z, YL, CORE, X, YH), ("z", "yl", "core", "x", "yh"))
    patch, head = ("z", "yl", "core"), ("x", "yh")
    tokens = P(patch + head, None)
    tiles = P(patch, head)
    return jax.shard_map(
        body,
        mesh=fine,
        in_specs=(tokens, tokens, tokens, tiles, tiles, P(), P()),
        out_specs=(tokens, tiles),
        check_vma=False,
    )
```

```python
import functools
import jax
import jax.numpy as jnp
from jax import lax
from jax.experimental import pallas as pl
from jax.experimental.pallas import tpu as pltpu
from jax.sharding import Mesh, PartitionSpec as P

HEADS = 24
HD = 128
EPSILON = 1e-06
LOG2E = 1.4426950408889634
SCALE2 = HD**-0.5 * LOG2E
BF = jnp.bfloat16
F32 = jnp.float32
LIMIT = 32 * 2**20
SMALL = 16 * 2**20
TOK, EXTRA = 48, 8


def norm(src, gain):
    values = src[...].astype(F32)
    mean = jnp.sum(values * values, axis=1, keepdims=True) / src.shape[1]
    return (values * lax.rsqrt(mean + EPSILON) * gain[...]).astype(BF)


def prep_q_kernel(copies, groups, q_ref, gain_ref, out_ref):
    per = q_ref.shape[1] // groups
    q = norm(q_ref, gain_ref)
    for g in range(groups):
        for c in range(copies):
            out_ref[c * groups + g] = q[:, g * per : (g + 1) * per]


def prep_kv_kernel(copies, groups, k_ref, v_ref, gain_ref, out_ref):
    per = k_ref.shape[1] // groups
    k = norm(k_ref, gain_ref)
    for g in range(groups):
        cols = slice(g * per, (g + 1) * per)
        out_ref[g, :, :per] = k[:, cols]
        out_ref[g, :, per:] = v_ref[:, cols]


def prep(kernel, name, copies, groups, gain, *sources):
    rows, width = sources[0].shape
    vmem = pl.BlockSpec(memory_space=pltpu.VMEM)
    return pl.pallas_call(
        functools.partial(kernel, copies, groups),
        out_shape=jax.ShapeDtypeStruct((copies * groups, rows, len(sources) * width // groups), BF),
        in_specs=[vmem] * (len(sources) + 1),
        out_specs=vmem,
        compiler_params=pltpu.CompilerParams(vmem_limit_bytes=SMALL),
        name=name,
    )(*sources, gain[None, :])


def attn_kernel(keys, spans, first, last, *refs):
    refs = list(refs)
    patches = len(spans)
    q_ref = refs.pop(0)
    blocks = [refs.pop(0) for _ in keys]
    states = [None if new else (refs.pop(0), refs.pop(0)) for new in first]
    yl_ref = refs.pop(0)
    place = [yl_ref[0], 1 - yl_ref[0]]
    if last:
        out_ref = refs.pop(0)
    else:
        results = [(refs.pop(0), refs.pop(0)) for _ in spans]
    q_buf, k_buf, v_buf, o_buf, lse_buf, sems, out_sem = refs
    nq, width = q_buf.shape
    heads = width // HD
    bq = nq // patches
    total = sum(keys)

    def start(src, dst, sem):
        copy = pltpu.make_async_copy(src, dst, sem)
        copy.start()
        return copy

    early, late = [], []
    off = 0
    for n, block in zip(keys, blocks):
        early.append(start(block.at[:, pl.ds(0, width)], k_buf.at[pl.ds(off, n)], sems.at[0]))
        off += n
    for i in range(patches):
        src = q_ref.at[pl.ds(pl.multiple_of(place[i] * bq, bq), bq)]
        early.append(start(src, q_buf.at[pl.ds(i * bq, bq)], sems.at[1]))
    off = 0
    for n, block in zip(keys, blocks):
        for h in range(heads):
            src = block.at[:, pl.ds(width + h * HD, HD)]
            late.append(start(src, v_buf.at[h, pl.ds(off, n), pl.ds(0, HD)], sems.at[2]))
        off += n
    for i, state in enumerate(states):
        if state is not None:
            rows = pl.ds(i * bq, bq)
            late.append(start(state[0], o_buf.at[rows], sems.at[3]))
            late.append(start(state[1], lse_buf.at[rows], sems.at[4]))
    for h in range(heads):
        v_buf[h, :, HD:] = jnp.ones((total, HD), BF)
    for copy in early:
        copy.wait()

    def window(i):
        return slice(sum(keys[: spans[i][0]]), sum(keys[: spans[i][1]]))

    def scores(work):
        h, i = work
        cols = slice(h * HD, (h + 1) * HD)
        q = q_buf[i * bq : (i + 1) * bq, cols]
        return lax.dot_general(q, k_buf[window(i), cols], (((1,), (1,)), ((), ())), preferred_element_type=F32)

    tok = TOK
    lane = lax.broadcasted_iota(jnp.int32, (bq, HD), 1)
    eye = lax.broadcasted_iota(jnp.int32, (tok, HD), 0) == lax.broadcasted_iota(jnp.int32, (tok, HD), 1)
    which = lax.broadcasted_iota(jnp.int32, (EXTRA, HD), 0)
    done = [None] * patches

    def rest(work, s):
        h, i = work
        rows, cols = slice(i * bq, (i + 1) * bq), slice(h * HD, (h + 1) * HD)
        m = jnp.max(s, axis=1, keepdims=True) * SCALE2
        if not first[i]:
            lse_old = lse_buf[rows][:, h : h + 1]
            m = jnp.maximum(lse_old, m)
        p = jnp.exp2(s * SCALE2 - m).astype(BF)
        o = jnp.dot(p, v_buf[h, window(i)], preferred_element_type=F32)
        a, l = o[:, :HD], o[:, HD:]
        if not first[i]:
            old = jnp.exp2(lse_old - m)
            a = a + o_buf[rows, cols].astype(F32) * old
            l = l + old
        o = (a / l).astype(BF)
        lse = m + jnp.log(l) * LOG2E
        if not last:
            o_buf[rows, cols] = o
            done[i] = lse if h == 0 else jnp.where(lane == h, lse, done[i])
            if h == heads - 1:
                lse_buf[rows] = done[i]
            return
        for t in range(bq // tok):
            d = place[i] * (bq // tok) + t
            row = jnp.sum(jnp.where(eye, lse[t * tok : (t + 1) * tok], 0.0), axis=0, keepdims=True)
            hi = row.astype(BF).astype(F32)
            mid = (row - hi).astype(BF).astype(F32)
            low = row - hi - mid
            packed = jnp.where(which == 0, hi, jnp.where(which == 1, mid, jnp.where(which == 2, low, 0.0)))
            out_ref[d, :, cols] = jnp.concatenate([o[t * tok : (t + 1) * tok], packed.astype(BF)], axis=0)

    pending = None
    for work in [(h, i) for h in range(heads) for i in range(patches)]:
        s = scores(work)
        if pending is None:
            for copy in late:
                copy.wait()
        else:
            rest(*pending)
        pending = (work, s)
    rest(*pending)
    if not last:
        stores = []
        for i, (o_hbm, lse_hbm) in enumerate(results):
            rows = pl.ds(i * bq, bq)
            stores.append(start(o_buf.at[rows], o_hbm, out_sem.at[0]))
            stores.append(start(lse_buf.at[rows], lse_hbm, out_sem.at[1]))
        for copy in stores:
            copy.wait()


def attend(q, yl, blocks, states=None, spans=None, last=False, name="attend"):
    nq, width = q.shape
    patches = YL
    bq = nq // patches
    heads = width // HD
    keys = tuple(b.shape[0] for b in blocks)
    states = states or [None] * patches
    spans = spans or [(0, len(keys))] * patches
    first = [s is None for s in states]
    total = sum(keys)
    hbm = pl.BlockSpec(memory_space=pl.ANY)
    args = [q, *blocks]
    alias = {}
    for i, state in enumerate(states):
        if state is not None:
            if not last:
                alias |= {len(args): 2 * i, len(args) + 1: 2 * i + 1}
            args += list(state)
    args.append(yl)
    specs = [hbm] * (len(args) - 1) + [pl.BlockSpec(memory_space=pltpu.SMEM)]
    if last:
        out_shape = jax.ShapeDtypeStruct((nq // TOK, TOK + EXTRA, width), BF)
        out_specs = pl.BlockSpec(memory_space=pltpu.VMEM)
    else:
        out_shape = [jax.ShapeDtypeStruct((bq, width), BF), jax.ShapeDtypeStruct((bq, HD), F32)] * patches
        out_specs = [hbm] * len(out_shape)
    seen = sum(sum(keys[a:b]) for a, b in spans)
    out = pl.pallas_call(
        functools.partial(attn_kernel, keys, spans, first, last),
        in_specs=specs,
        out_specs=out_specs,
        out_shape=out_shape,
        scratch_shapes=[
            pltpu.VMEM((nq, width), BF),
            pltpu.VMEM((total, width), BF),
            pltpu.VMEM((heads, total, 2 * HD), BF),
            pltpu.VMEM((nq, width), BF),
            pltpu.VMEM((nq, HD), F32),
            pltpu.SemaphoreType.DMA((5,)),
            pltpu.SemaphoreType.DMA((2,)),
        ],
        input_output_aliases=alias,
        compiler_params=pltpu.CompilerParams(vmem_limit_bytes=LIMIT),
        cost_estimate=pl.CostEstimate(flops=4 * bq * seen * width, bytes_accessed=2**20, transcendentals=bq * seen * heads),
        name=name,
    )(*args)
    return out if last else [out[2 * i : 2 * i + 2] for i in range(patches)]


def merge_kernel(groups, copies, in_ref, out_ref):
    tok = TOK
    heads = in_ref.shape[2] // HD
    eye = lax.broadcasted_iota(jnp.int32, (tok, HD), 0) == lax.broadcasted_iota(jnp.int32, (tok, HD), 1)
    for g in range(groups):
        for h in range(heads):
            cols = slice(h * HD, (h + 1) * HD)
            parts = [in_ref[c * groups + g, :, cols].astype(F32) for c in range(copies)]
            lses = []
            for part in parts:
                row = jnp.sum(part[tok:], axis=0, keepdims=True)
                lses.append(jnp.sum(jnp.where(eye, jnp.broadcast_to(row, (tok, HD)), 0.0), axis=1, keepdims=True))
            top = functools.reduce(jnp.maximum, lses)
            weights = [jnp.exp2(x - top) for x in lses]
            total = sum(weights)
            acc = sum(part[:tok] * (weight / total) for part, weight in zip(parts, weights))
            first = (g * heads + h) * HD
            out_ref[:, first : first + HD] = acc.astype(BF)


def merge(parts, groups, copies):
    width = parts.shape[2] * groups
    return pl.pallas_call(
        functools.partial(merge_kernel, groups, copies),
        out_shape=jax.ShapeDtypeStruct((TOK, width), BF),
        in_specs=[pl.BlockSpec(memory_space=pltpu.VMEM)],
        out_specs=pl.BlockSpec(memory_space=pltpu.VMEM),
        compiler_params=pltpu.CompilerParams(vmem_limit_bytes=SMALL),
        name="merge",
    )(parts)


Z, YL, CORE, X, YH = 8, 2, 2, 4, 2
UP = [(i, (i + 1) % Z) for i in range(Z)]
DOWN = [(i, (i - 1) % Z) for i in range(Z)]
SWAP = [(0, 1), (1, 0)]


def other_core(x):
    return lax.ppermute(x, "core", SWAP)


def body(fresh_q, fresh_k, fresh_v, stale_k, stale_v, q_gain, k_gain):
    groups = X * YH
    width_dev = stale_k.shape[1]
    half = stale_k.shape[0] // 2
    yl = lax.axis_index("yl").astype(jnp.int32).reshape(1)

    def both(pair):
        return lax.ppermute(pair[0], "z", UP), lax.ppermute(pair[1], "z", DOWN)

    def swap(pair):
        return other_core(pair[0]), other_core(pair[1])

    own = jnp.concatenate([stale_k, stale_v], axis=1)
    r1 = both((own, own))
    q_parts = prep(prep_q_kernel, "prep_q", YL, groups, q_gain, fresh_q)
    q = lax.all_to_all(q_parts, ("yl", "x", "yh"), split_axis=0, concat_axis=0, tiled=True)
    kv_parts = prep(prep_kv_kernel, "prep_kv", 1, groups, k_gain, fresh_k, fresh_v)
    down1, q, kv_parts = lax.optimization_barrier((r1[1], q, kv_parts))
    r1 = (r1[0], down1)
    q = q.reshape(-1, width_dev)
    r2 = both(r1)
    fresh = lax.all_to_all(kv_parts, ("x", "yh"), split_axis=0, concat_axis=0, tiled=True)
    own_other = other_core(own)
    state = attend(q, yl, [*r1, *swap(r1)], name="attend1")
    r2, state = lax.optimization_barrier((r2, state))

    r3 = both(r2)
    r2, fresh = lax.optimization_barrier((r2, fresh))
    fresh = fresh.reshape(-1, 2 * width_dev)
    blocks = [own, own_other, *r2, *swap(r2), fresh]
    state = attend(q, yl, blocks, state, [(1, 7), (0, 6)], name="attend2")
    r3, state = lax.optimization_barrier((r3, state))
    r4 = both((r3[0][:half], r3[1][half:]))
    state = attend(q, yl, [*r3, *swap(r3)], state, name="attend3")
    r4, state = lax.optimization_barrier((r4, state))
    parts = attend(q, yl, [*r4, *swap(r4)], state, last=True, name="attend4")
    back = lax.all_to_all(parts, ("yl", "x", "yh"), split_axis=0, concat_axis=0, tiled=True)
    return merge(back, groups, YL), fresh[:, :width_dev]


def solution(mesh):
    fine = Mesh(mesh.devices.reshape(Z, YL, CORE, X, YH), ("z", "yl", "core", "x", "yh"))
    patch, head = ("z", "yl", "core"), ("x", "yh")
    tokens = P(patch + head, None)
    tiles = P(patch, head)
    return jax.shard_map(
        body,
        mesh=fine,
        in_specs=(tokens, tokens, tokens, tiles, tiles, P(), P()),
        out_specs=(tokens, tiles),
        check_vma=False,
    )
```
